256 devices in a mesh: row: 8 (over y, core), col: 32 (over z, x).
Axes of the slice: x: 4, y: 4, z: 8, core: 2. Of those that a mesh axis runs over, the one named last changes fastest.
Arguments:
- act_values: bfloat16 [1024, 12288], P('row', 'col'), may hold values from -6 to 6
- act_scales: float32 [1024, 96], P('row', 'col'), may hold values from 0.25 to 4
- weight_values: bfloat16 [12288, 12288], P('row', 'col'), may hold values from -0.0546875 to 0.0546875
- weight_scales: float32 [96, 96], P('row', 'col'), may hold values from 0.5 to 2
- cotangent: bfloat16 [1024, 12288], P('row', 'col'), may hold values from -6 to 6
Outputs:
- output: bfloat16 [1024, 12288], P('row', 'col')
- activation_grad: bfloat16 [1024, 12288], P('row', 'col')
- weight_grad: float32 [12288, 12288], P('row', 'col')
The draws below stay inside these ranges and needn't reach their ends.
All inputs are finite; a program needn't handle non-finite values.
Results may differ from the reference program's by a relative error of at most 0.0057.
Values may be sent and summed in bfloat16 or wider, within the bound.
No kernel may reach another device: no remote copies, remote signals or barrier semaphores. Data moves between devices by JAX's collectives and lax.ppermute only.
A program may use at most 128 MiB of HBM per device.

```python
import math
import jax
import jax.numpy as jnp
from jax import lax

D = 12288
BLOCK = 128
TOKENS = 1024


def steps_of(rng, dims, shards, smallest, largest):
    def one(axis_at, parts):
        draws = jax.random.uniform(jax.random.fold_in(jax.random.fold_in(rng, 6), axis_at), (parts,), jnp.float32, smallest / len(shards), largest / len(shards))
        return jnp.repeat(jnp.exp(draws), dims[axis_at] // parts).reshape((-1,) + (1,) * (len(dims) - axis_at - 1))

    loudness = one(*shards[0])
    for cut in shards[1:]:
        loudness = loudness * one(*cut)
    return loudness


def gaussian(rng, extent, spread, reach, cuts=(), held_as=jnp.bfloat16):
    values = spread * jax.random.normal(rng, extent, jnp.float32)
    if cuts:
        values = values * steps_of(rng, extent, cuts, -0.22, 0.18)
    return jnp.clip(values, -reach, reach).astype(held_as)


def setup_inputs(seed: int = 0) -> dict:
    key_list = jax.random.split(jax.random.key(seed), 6)
    act_values = gaussian(key_list[0], (TOKENS, D), 1.0, 6.0, ((0, 8), (1, 32)))
    act_scales = jnp.clip(jnp.exp(math.log(4.0) - 2.7725887 * jax.random.uniform(key_list[1], (TOKENS, D // BLOCK), jnp.float32) ** steps_of(key_list[1], (TOKENS, D // BLOCK), ((0, 8), (1, 32)), -0.2, 0.2)), 0.25, 4.0)
    weight_values = gaussian(key_list[2], (D, D), D ** -0.5, 0.0546875, ((0, 8), (1, 32)))
    weight_scales = jnp.clip(jnp.exp(math.log(2.0) - 1.3862944 * jax.random.uniform(key_list[3], (D // BLOCK, D // BLOCK), jnp.float32) ** steps_of(key_list[3], (D // BLOCK, D // BLOCK), ((0, 8), (1, 32)), -0.2, 0.2)), 0.5, 2.0)
    cotangent = gaussian(key_list[4], (TOKENS, D), 1.0, 6.0, ((0, 8), (1, 32)))
    return dict(act_values=act_values, act_scales=act_scales, weight_values=weight_values, weight_scales=weight_scales, cotangent=cotangent)


def dequantize_rows(values, scales):
    blocks = values.astype(jnp.float32).reshape(values.shape[0], scales.shape[1], -1) * scales[:, :, None]
    return blocks.reshape(values.shape).astype(jnp.bfloat16)


def dequantize_tile(values, scales):
    blocks = values.astype(jnp.float32).reshape(scales.shape[0], -1, scales.shape[1], values.shape[1] // scales.shape[1])
    blocks = blocks * scales[:, None, :, None]
    return blocks.reshape(values.shape).astype(jnp.bfloat16)


def reference(act_values, act_scales, weight_values, weight_scales, cotangent):
    activations = dequantize_rows(act_values, act_scales)
    weight = dequantize_tile(weight_values, weight_scales)
    output = jnp.dot(activations, weight, preferred_element_type=jnp.float32).astype(jnp.bfloat16)
    activation_grad = lax.dot_general(cotangent, weight, (((1,), (1,)), ((), ())), preferred_element_type=jnp.float32).astype(jnp.bfloat16)
    weight_grad = lax.dot_general(activations, cotangent, (((0,), (0,)), ((), ())), preferred_element_type=jnp.float32)
    weight_grad = weight_grad * (float(TOKENS) ** -0.5)
    return (output, activation_grad, weight_grad)
```

```python
import jax
import jax.numpy as jnp
from jax import lax
from jax.sharding import PartitionSpec as P

NY, NC, NZ, NX = 4, 2, 8, 4
NR = NY * NC
SKEW = (0, 4, 1, 5, 2, 6, 3, 7)
UNSKEW = tuple(SKEW.index(i) for i in range(NZ))
BF, F32 = jnp.bfloat16, jnp.float32


def dequantize_rows(values, scales):
    blocks = (
        values.astype(F32).reshape(values.shape[0], scales.shape[1], -1)
        * scales[:, :, None]
    )
    return blocks.reshape(values.shape).astype(BF)


def dequantize_tile(values, scales):
    blocks = values.astype(F32).reshape(
        scales.shape[0], -1, scales.shape[1], values.shape[1] // scales.shape[1]
    )
    blocks = blocks * scales[:, None, :, None]
    return blocks.reshape(values.shape).astype(BF)


def move(value, where):
    pairs = []
    for r in range(NR):
        for z in range(NZ):
            for x in range(NX):
                r2, z2, x2 = where(r, z, x)
                pairs.append(
                    (
                        (r * NZ + z) * NX + x,
                        ((r2 % NR) * NZ + z2 % NZ) * NX + x2 % NX,
                    )
                )
    return lax.ppermute(value, ("row", "col"), pairs)


def along_x(value, k):
    return move(value, lambda r, z, x: (r, z, x + k))


def along_z(value, k):
    return move(value, lambda r, z, x: (r, z + k, x))


def along_y(value, k):
    return move(value, lambda r, z, x: (r + NC * k, z, x))


def other_core(value):
    return move(value, lambda r, z, x: (r ^ 1, z, x))


def mm(a, b):
    return jnp.dot(a, b, preferred_element_type=F32)


def mm_t(a, b):
    return lax.dot_general(a, b, (((1,), (1,)), ((), ())), preferred_element_type=F32)


def per_device(act_values, act_scales, weight_values, weight_scales, cotangent):
    r = lax.axis_index("row")
    col = lax.axis_index("col")
    z, x = col // NX, col % NX
    t, n = cotangent.shape

    act = dequantize_rows(act_values, act_scales)
    here = move(act, lambda r, z, x: (z, z + SKEW[r], x))
    cots = [cotangent, along_y(cotangent, 1), along_y(cotangent, -1), along_y(cotangent, 2)]
    wide = jnp.zeros((t, NX, n), BF)
    parts = [here, along_x(here, 1), along_x(here, -1), along_x(here, 2)]
    for part, off in zip(parts, (0, 3, 1, 2)):
        wide = lax.dynamic_update_slice(wide, part[:, None, :], (0, (x + off) % NX, 0))
    block = wide.reshape(t, NX * n)

    near = jnp.stack(cots)
    cot_rows = jnp.concatenate([near, other_core(near)])
    steps = jnp.arange(NZ)
    rows = jnp.array(UNSKEW)[(z + steps - r) % NZ]
    apart = (rows // NC - r // NC) % NY
    slot = jnp.array((0, 2, 3, 1))[apart] + jnp.where(rows % NC == r % NC, 0, NY)
    cot = jnp.take(cot_rows, slot, axis=0).reshape(NZ * t, n)

    weight = dequantize_tile(weight_values, weight_scales)
    by_x = weight.reshape(NX, n, n)

    def rows_of(off):
        return lax.dynamic_index_in_dim(by_x, (x + off) % NX, keepdims=False)

    half = NZ * t // 2
    lo, hi = cot[:half], cot[half:]
    w_far, w_right, w_left = rows_of(2), rows_of(1), rows_of(3)
    far_lo = along_x(mm_t(lo, w_far).astype(BF), 1)
    far_hi = along_x(mm_t(hi, w_far).astype(BF), -1)
    right_hi = along_x(mm_t(hi, w_right).astype(BF), 1)
    left_lo = along_x(mm_t(lo, w_left).astype(BF), -1)
    right_lo = along_x((mm_t(lo, w_right) + far_lo.astype(F32)).astype(BF), 1)
    left_hi = along_x((mm_t(hi, w_left) + far_hi.astype(F32)).astype(BF), -1)
    w_here = rows_of(0)
    sum_lo = mm_t(lo, w_here) + right_lo.astype(F32) + left_lo.astype(F32)
    sum_hi = mm_t(hi, w_here) + right_hi.astype(F32) + left_hi.astype(F32)

    def grad(s):
        of, at = (sum_lo, s) if s < NZ // 2 else (sum_hi, s - NZ // 2)
        return of[at * t : (at + 1) * t]

    up = along_z(grad(4).astype(BF), 1)
    down = along_z(grad(5).astype(BF), -1)
    for s in (3, 2, 1):
        up = along_z((grad(s) + up.astype(F32)).astype(BF), 1)
        if s > 1:
            down = along_z((grad(9 - s) + down.astype(F32)).astype(BF), -1)
    total = grad(0) + up.astype(F32) + down.astype(F32)
    activation_grad = move(
        total.astype(BF), lambda r, z, x: (UNSKEW[(z - r) % NZ], r, x)
    )

    blocks = [None] * NZ
    blocks[0] = block
    for s in range(1, NZ // 2 + 1):
        blocks[s] = along_z(blocks[s - 1], -1)
        if s < NZ // 2:
            blocks[NZ - s] = along_z(blocks[(NZ - s + 1) % NZ], 1)
    output = 0
    for s in range(NZ):
        share = mm(blocks[s], weight).astype(BF)
        share = move(share, lambda r, z, x: (UNSKEW[(z + s - r) % NZ], z, x))
        output = output + share.astype(F32)
    output = output.astype(BF)

    weight_grad = lax.dot_general(
        jnp.concatenate(blocks),
        cot,
        (((0,), (0,)), ((), ())),
        preferred_element_type=F32,
    )
    weight_grad = weight_grad * float(NR * t) ** (-0.5)
    return output, activation_grad, weight_grad


def solution(mesh):
    spec = P("row", "col")
    return jax.shard_map(
        per_device,
        mesh=mesh,
        in_specs=(spec,) * 5,
        out_specs=(spec,) * 3,
        check_vma=False,
    )
```

```python
import jax
import jax.numpy as jnp
from jax import lax
from jax.experimental import pallas as pl
from jax.experimental.pallas import tpu as pltpu
from jax.sharding import Mesh
from jax.sharding import PartitionSpec as P

NR, NC, NZ, NX = 8, 2, 8, 4
BF, F32 = jnp.bfloat16, jnp.float32
VMEM = 48 * 1024 * 1024


def dequantize_rows(values, scales):
    blocks = (
        values.astype(F32).reshape(values.shape[0], scales.shape[1], -1)
        * scales[:, :, None]
    )
    return blocks.reshape(values.shape).astype(BF)


def skew(r):
    return r // NC + r % NC * (NR // NC)


def unskew(d):
    d = d % NZ
    return d % (NR // NC) * NC + d // (NR // NC)


def move(value, where):
    pairs = []
    for r in range(NR):
        for z in range(NZ):
            for x in range(NX):
                r2, z2, x2 = where(r, z, x)
                to = ((r2 % NR) * NZ + z2 % NZ) * NX + x2 % NX
                pairs.append(((r * NZ + z) * NX + x, to))
    return lax.ppermute(value, ("r", "z", "x"), pairs)


def along_x(value, k):
    return move(value, lambda r, z, x: (r, z, x + k))


def along_z(value, k):
    return move(value, lambda r, z, x: (r, z + k, x))


def mm(a, b):
    return jnp.dot(a, b, preferred_element_type=F32)


def grad_kernel(scales, cot, values, parts, weight):
    at = pl.program_id(0)
    size = 128
    for i in range(values.shape[0] // size):
        for j in range(values.shape[1] // size):
            rows, cols = pl.ds(i * size, size), pl.ds(j * size, size)
            scale = scales[at * (values.shape[0] // size) + i, j]
            weight[rows, cols] = (values[rows, cols].astype(F32) * scale).astype(BF)
    part = lax.dot_general(
        cot[...], weight[...], (((1,), (1,)), ((), ())), preferred_element_type=F32
    )
    parts[...] = part.astype(BF).reshape(parts.shape)


def grad_parts(cot, values, scales):
    t, n = cot.shape
    k = values.shape[0]
    rows = t // NR
    return pl.pallas_call(
        grad_kernel,
        grid=(NX,),
        out_shape=(
            jax.ShapeDtypeStruct((NR, NX, rows, k // NX), BF),
            jax.ShapeDtypeStruct((k, n), BF),
        ),
        in_specs=[
            pl.BlockSpec(memory_space=pltpu.SMEM),
            pl.BlockSpec((t, n), lambda i: (0, 0)),
            pl.BlockSpec((k // NX, n), lambda i: (i, 0)),
        ],
        out_specs=(
            pl.BlockSpec((NR, 1, rows, k // NX), lambda i: (0, i, 0, 0)),
            pl.BlockSpec((k // NX, n), lambda i: (i, 0)),
        ),
        compiler_params=pltpu.CompilerParams(vmem_limit_bytes=VMEM),
        cost_estimate=pl.CostEstimate(
            flops=2 * t * n * k, bytes_accessed=2 * t * k, transcendentals=0
        ),
    )(scales, cot, values)


def sum_kernel(z, parts, out):
    for s in range(NZ):
        at = lax.rem(z[0] + s, NZ)
        total = parts[at, 0].astype(F32)
        for i in range(1, NX):
            total = total + parts[at, i].astype(F32)
        out[s] = total


def sum_over_x(z, parts):
    _, _, rows, k = parts.shape
    return pl.pallas_call(
        sum_kernel,
        out_shape=jax.ShapeDtypeStruct((NZ, rows, k), F32),
        in_specs=[
            pl.BlockSpec(memory_space=pltpu.SMEM),
            pl.BlockSpec(memory_space=pltpu.VMEM),
        ],
        out_specs=pl.BlockSpec(memory_space=pltpu.VMEM),
        compiler_params=pltpu.CompilerParams(vmem_limit_bytes=VMEM),
        cost_estimate=pl.CostEstimate(
            flops=NZ * NX * rows * k, bytes_accessed=12 * NZ * rows * k, transcendentals=0
        ),
    )(z.reshape(1), parts)


def assemble_kernel(x, *refs):
    parts, out = refs[:NX], refs[NX]
    n = parts[0].shape[1]
    for off in range(NX):
        at = pl.multiple_of(lax.rem(x[0] + off, NX) * n, 128)
        out[:, pl.ds(at, n)] = parts[off][...]


def assemble(x, parts):
    t, n = parts[0].shape
    return pl.pallas_call(
        assemble_kernel,
        out_shape=jax.ShapeDtypeStruct((t, NX * n), BF),
        in_specs=[pl.BlockSpec(memory_space=pltpu.SMEM)]
        + [pl.BlockSpec(memory_space=pltpu.VMEM)] * NX,
        out_specs=pl.BlockSpec(memory_space=pltpu.VMEM),
        cost_estimate=pl.CostEstimate(
            flops=0, bytes_accessed=4 * t * NX * n, transcendentals=0
        ),
    )(x.reshape(1), *parts)


def together(*values):
    return lax.optimization_barrier(values)


def per_device(act_values, act_scales, weight_values, weight_scales, cotangent):
    r, z, x = (lax.axis_index(a) for a in ("r", "z", "x"))
    t, n = cotangent.shape

    act = dequantize_rows(act_values, act_scales)
    act, cotangent = together(act, cotangent)
    here = move(act, lambda r, z, x: (z, z + skew(r), x))
    cot = lax.all_gather(cotangent, "r", axis=0, tiled=True)
    here, cot = together(here, cot)

    sides = [along_x(here, -1), along_x(here, 2), along_x(here, 1)]
    parts, weight = grad_parts(cot, weight_values, weight_scales)
    parts, *sides = together(parts, *sides)
    parts = lax.all_to_all(
        parts.reshape(NR * NX, t, n), ("r", "x"), split_axis=0, concat_axis=0, tiled=True
    )

    blocks = {0: assemble(x, [here, *sides])}
    for s in range(1, NZ // 2 + 1):
        blocks[s] = along_z(blocks[s - 1], -1)
        if s < NZ // 2:
            blocks[NZ - s] = along_z(blocks[(NZ - s + 1) % NZ], 1)
    shares = jnp.zeros((NR, t, n), BF)
    for s in (0, 1, 7, 2, 6, 3, 5, 4):
        part = mm(blocks[s], weight).astype(BF)
        shares = lax.dynamic_update_slice(
            shares, part[None], (unskew(z + s - r), 0, 0)
        )
    shares = lax.all_to_all(shares, "r", split_axis=0, concat_axis=0, tiled=True)
    output = jnp.sum(shares.astype(F32), axis=0).astype(BF)

    sums = sum_over_x(z, parts.reshape(NZ, NX, t, n))
    low = sums.astype(BF)
    across = along_z(low[4], 4)
    up = along_z(jnp.stack([low[1], low[3]]), 1)
    down = along_z(jnp.stack([low[7], low[5]]), -1)
    up, down = up.astype(F32), down.astype(F32)
    up2 = along_z((sums[2] + up[1]).astype(BF), 2)
    down2 = along_z((sums[6] + down[1]).astype(BF), -2)
    total = sums[0] + up[0] + down[0] + across.astype(F32)
    activation_grad = (total + up2.astype(F32) + down2.astype(F32)).astype(BF)

    cot, _ = together(cot, blocks[1])
    cot = cot.reshape(NR, t, n)
    cot = jnp.concatenate(
        [
            lax.dynamic_index_in_dim(cot, unskew(z + s - r), keepdims=False)
            for s in range(NZ)
        ]
    )
    weight_grad = lax.dot_general(
        jnp.concatenate([blocks[s] for s in range(NZ)]),
        cot,
        (((0,), (0,)), ((), ())),
        preferred_element_type=F32,
    )
    weight_grad = weight_grad * float(NR * t) ** (-0.5)
    return output, activation_grad, weight_grad


def solution(mesh):
    grid = Mesh(mesh.devices.reshape(NR, NZ, NX), ("r", "z", "x"))
    spec = P("r", ("z", "x"))
    return jax.shard_map(
        per_device,
        mesh=grid,
        in_specs=(spec,) * 5,
        out_specs=(spec,) * 3,
        check_vma=False,
    )
```

```python
import jax
import jax.numpy as jnp
from jax import lax
from jax.experimental import pallas as pl
from jax.experimental.pallas import tpu as pltpu
from jax.sharding import Mesh
from jax.sharding import PartitionSpec as P

NR, NC, NY, NZ, NX = 8, 2, 4, 8, 4
BF, F32 = jnp.bfloat16, jnp.float32
BLOCK = 128
VMEM = 16 * 1024 * 1024


def dequantize_rows(values, scales):
    blocks = (
        values.astype(F32).reshape(values.shape[0], scales.shape[1], -1)
        * scales[:, :, None]
    )
    return blocks.reshape(values.shape).astype(BF)


def skew(r):
    return r // NC + r % NC * (NR // NC)


def unskew(d):
    d = d % NZ
    return d % (NR // NC) * NC + d // (NR // NC)


def move(value, where):
    pairs = []
    for r in range(NR):
        for z in range(NZ):
            for x in range(NX):
                r2, z2, x2 = where(r, z, x)
                to = ((r2 % NR) * NZ + z2 % NZ) * NX + x2 % NX
                pairs.append(((r * NZ + z) * NX + x, to))
    return lax.ppermute(value, ("r", "z", "x"), pairs)


def along_x(value, k):
    return move(value, lambda r, z, x: (r, z, x + k))


def along_y(value, k):
    return move(value, lambda r, z, x: (r + NC * k, z, x))


def along_z(value, k):
    return move(value, lambda r, z, x: (r, z + k, x))


def mm(a, b):
    return jnp.dot(a, b, preferred_element_type=F32)


def grad_kernel(place, scales, near, far, values, parts, weight, cot):
    at = pl.program_id(0)
    for i in range(values.shape[0] // BLOCK):
        for j in range(values.shape[1] // BLOCK):
            rows, cols = pl.ds(i * BLOCK, BLOCK), pl.ds(j * BLOCK, BLOCK)
            scale = scales[at * (values.shape[0] // BLOCK) + i, j]
            weight[rows, cols] = (values[rows, cols].astype(F32) * scale).astype(BF)
    half, rows, n = near.shape
    for h, some in enumerate((near, far)):
        part = lax.dot_general(
            some[...].reshape(half * rows, n),
            weight[...],
            (((1,), (1,)), ((), ())),
            preferred_element_type=F32,
        ).astype(BF)
        for i in range(half):
            parts[place[h * half + i], 0] = part[i * rows : (i + 1) * rows]

    @pl.when(at == 0)
    def _():
        for h, some in enumerate((near, far)):
            for i in range(half):
                cot[place[NR + h * half + i]] = some[i]


def grad_parts(place, near, far, values, scales):
    half, rows, n = near.shape
    k = values.shape[0]
    whole = pl.BlockSpec((half, rows, n), lambda i: (0, 0, 0))
    scalars = pl.BlockSpec(memory_space=pltpu.SMEM)
    return pl.pallas_call(
        grad_kernel,
        grid=(NX,),
        out_shape=(
            jax.ShapeDtypeStruct((NR, NX, rows, k // NX), BF),
            jax.ShapeDtypeStruct((k, n), BF),
            jax.ShapeDtypeStruct((NR, rows, n), BF),
        ),
        in_specs=[
            scalars,
            scalars,
            whole,
            whole,
            pl.BlockSpec((k // NX, n), lambda i: (i, 0)),
        ],
        out_specs=(
            pl.BlockSpec((NR, 1, rows, k // NX), lambda i: (0, i, 0, 0)),
            pl.BlockSpec((k // NX, n), lambda i: (i, 0)),
            pl.BlockSpec((NR, rows, n), lambda i: (0, 0, 0)),
        ),
        compiler_params=pltpu.CompilerParams(vmem_limit_bytes=VMEM),
        cost_estimate=pl.CostEstimate(
            flops=4 * half * rows * n * k,
            bytes_accessed=4 * half * rows * k,
            transcendentals=0,
        ),
    )(place, scales, near, far, values)


def sum_kernel(z, parts, ahead, behind, across, kept):
    def of(s):
        at = lax.rem(z[0] + s, NZ)
        total = parts[at, 0].astype(F32)
        for i in range(1, NX):
            total = total + parts[at, i].astype(F32)
        return total

    for i, (near, far) in enumerate(((1, 7), (3, 5))):
        ahead[i] = of(near).astype(BF)
        behind[i] = of(far).astype(BF)
    across[...] = of(4).astype(BF)
    for i, s in enumerate((0, 2, 6)):
        kept[i] = of(s)


def sum_over_x(z, parts):
    _, _, rows, k = parts.shape
    vmem = pl.BlockSpec(memory_space=pltpu.VMEM)
    return pl.pallas_call(
        sum_kernel,
        out_shape=(
            jax.ShapeDtypeStruct((2, rows, k), BF),
            jax.ShapeDtypeStruct((2, rows, k), BF),
            jax.ShapeDtypeStruct((rows, k), BF),
            jax.ShapeDtypeStruct((3, rows, k), F32),
        ),
        in_specs=[pl.BlockSpec(memory_space=pltpu.SMEM), vmem],
        out_specs=(vmem,) * 4,
        compiler_params=pltpu.CompilerParams(vmem_limit_bytes=VMEM),
        cost_estimate=pl.CostEstimate(
            flops=NZ * NX * rows * k, bytes_accessed=12 * NZ * rows * k, transcendentals=0
        ),
    )(z.reshape(1), parts)


def assemble_kernel(x, *refs):
    parts, out = refs[:NX], refs[NX]
    n = parts[0].shape[1]
    for off in range(NX):
        at = pl.multiple_of(lax.rem(x[0] + off, NX) * n, 128)
        out[:, pl.ds(at, n)] = parts[off][...]


def assemble(x, parts):
    t, n = parts[0].shape
    return pl.pallas_call(
        assemble_kernel,
        out_shape=jax.ShapeDtypeStruct((t, NX * n), BF),
        in_specs=[pl.BlockSpec(memory_space=pltpu.SMEM)]
        + [pl.BlockSpec(memory_space=pltpu.VMEM)] * NX,
        out_specs=pl.BlockSpec(memory_space=pltpu.VMEM),
        cost_estimate=pl.CostEstimate(
            flops=0, bytes_accessed=4 * t * NX * n, transcendentals=0
        ),
    )(x.reshape(1), *parts)


def together(*values):
    return lax.optimization_barrier(values)


def per_device(act_values, act_scales, weight_values, weight_scales, cotangent):
    r, z, x = (lax.axis_index(a) for a in ("r", "z", "x"))
    t, n = cotangent.shape

    act = dequantize_rows(act_values, act_scales)
    act, cotangent = together(act, cotangent)
    here = move(act, lambda r, z, x: (z, z + skew(r), x))

    turns = (0, 1, -1, 2)
    near = jnp.stack([along_y(cotangent, -k) if k else cotangent for k in turns])
    near, here = together(near, here)
    far = move(near, lambda r, z, x: (r ^ 1, z, x))
    rows = [(r + NC * k) % NR ^ other for other in (0, 1) for k in turns]
    place = jnp.stack(rows + [(r + skew(row) - z) % NZ for row in rows])

    sides = [along_x(here, -1), along_x(here, 2), along_x(here, 1)]
    parts, weight, cot = grad_parts(place, near, far, weight_values, weight_scales)
    parts, *sides = together(parts, *sides)
    parts = lax.all_to_all(
        parts.reshape(NR * NX, t, n), ("r", "x"), split_axis=0, concat_axis=0, tiled=True
    )

    blocks = {0: assemble(x, [here, *sides])}
    for s in range(1, NZ // 2 + 1):
        blocks[s] = along_z(blocks[s - 1], -1)
        if s < NZ // 2:
            blocks[NZ - s] = along_z(blocks[(NZ - s + 1) % NZ], 1)
    shares = jnp.zeros((NR, t, n), BF)
    for s in (0, 1, 7, 2, 6, 3, 5, 4):
        part = mm(blocks[s], weight).astype(BF)
        row = unskew(z + s - r)
        at = (row // NC - r // NC) % NY + (row % NC ^ r % NC) * NY
        shares = lax.dynamic_update_slice(shares, part[None], (at, 0, 0))
    both = move(shares[NY:], lambda r, z, x: (r ^ 1, z, x)).astype(F32)
    both = shares[:NY].astype(F32) + both

    ahead, behind, across, kept = sum_over_x(z, parts.reshape(NZ, NX, t, n))
    up, down, across = along_z(ahead, 1), along_z(behind, -1), along_z(across, 4)
    up2 = along_z((kept[1] + up[1].astype(F32)).astype(BF), 2)
    down2 = along_z((kept[2] + down[1].astype(F32)).astype(BF), -2)
    total = kept[0] + up[0].astype(F32) + down[0].astype(F32) + across.astype(F32)
    activation_grad = (total + up2.astype(F32) + down2.astype(F32)).astype(BF)

    parts = [along_y(both[k].astype(BF), k) for k in range(1, NY)]
    output = (both[0] + sum(part.astype(F32) for part in parts)).astype(BF)

    cot = cot.reshape(NZ, t, n)

    def grad_of(some):
        return lax.dot_general(
            jnp.concatenate([blocks[s] for s in some]),
            jnp.concatenate([cot[s] for s in some]),
            (((0,), (0,)), ((), ())),
            preferred_element_type=F32,
        )

    first = (0, 1, 7, 2, 6, 3, 5)
    for s, block in zip(first, together(*(blocks[s] for s in first))):
        blocks[s] = block
    weight_grad = grad_of(first)
    weight_grad, blocks[4] = together(weight_grad, blocks[4])
    weight_grad = (weight_grad + grad_of((4,))) * float(NR * t) ** (-0.5)
    return output, activation_grad, weight_grad


def solution(mesh):
    grid = Mesh(mesh.devices.reshape(NR, NZ, NX), ("r", "z", "x"))
    spec = P("r", ("z", "x"))
    return jax.shard_map(
        per_device,
        mesh=grid,
        in_specs=(spec,) * 5,
        out_specs=(spec,) * 3,
        check_vma=False,
    )
```

```python
import jax
import jax.numpy as jnp
from jax import lax
from jax.experimental import pallas as pl
from jax.experimental.pallas import tpu as pltpu
from jax.sharding import Mesh
from jax.sharding import PartitionSpec as P

NR, NC, NY, NZ, NX = 8, 2, 4, 8, 4
BF, F32 = jnp.bfloat16, jnp.float32
BLOCK = 128
VMEM = 16 * 1024 * 1024


def dequantize_rows(values, scales):
    blocks = (
        values.astype(F32).reshape(values.shape[0], scales.shape[1], -1)
        * scales[:, :, None]
    )
    return blocks.reshape(values.shape).astype(BF)


def skew(r):
    return r // NC + r % NC * (NR // NC)


def unskew(d):
    d = d % NZ
    return d % (NR // NC) * NC + d // (NR // NC)


def move(value, where):
    pairs = []
    for r in range(NR):
        for z in range(NZ):
            for x in range(NX):
                r2, z2, x2 = where(r, z, x)
                to = ((r2 % NR) * NZ + z2 % NZ) * NX + x2 % NX
                pairs.append(((r * NZ + z) * NX + x, to))
    return lax.ppermute(value, ("r", "z", "x"), pairs)


def along_x(value, k):
    return move(value, lambda r, z, x: (r, z, x + k))


def along_y(value, k):
    return move(value, lambda r, z, x: (r + NC * k, z, x))


def along_z(value, k):
    return move(value, lambda r, z, x: (r, z + k, x))


def mm(a, b):
    return jnp.dot(a, b, preferred_element_type=F32)


def grad_kernel(place, scales, near, far, values, parts, weight, cot):
    at = pl.program_id(0)
    for i in range(values.shape[0] // BLOCK):
        for j in range(values.shape[1] // BLOCK):
            rows, cols = pl.ds(i * BLOCK, BLOCK), pl.ds(j * BLOCK, BLOCK)
            scale = scales[at * (values.shape[0] // BLOCK) + i, j]
            weight[rows, cols] = (values[rows, cols].astype(F32) * scale).astype(BF)
    half, rows, n = near.shape
    for h, some in enumerate((near, far)):
        part = lax.dot_general(
            some[...].reshape(half * rows, n),
            weight[...],
            (((1,), (1,)), ((), ())),
            preferred_element_type=F32,
        ).astype(BF)
        for i in range(half):
            parts[place[h * half + i], 0] = part[i * rows : (i + 1) * rows]

    @pl.when(at == 0)
    def _():
        for h, some in enumerate((near, far)):
            for i in range(half):
                cot[place[NR + h * half + i]] = some[i]


def grad_parts(place, near, far, values, scales):
    half, rows, n = near.shape
    k = values.shape[0]
    whole = pl.BlockSpec((half, rows, n), lambda i: (0, 0, 0))
    scalars = pl.BlockSpec(memory_space=pltpu.SMEM)
    return pl.pallas_call(
        grad_kernel,
        grid=(NX,),
        out_shape=(
            pltpu.HBM((NR, NX, rows, k // NX), BF),
            jax.ShapeDtypeStruct((k, n), BF),
            jax.ShapeDtypeStruct((NR, rows, n), BF),
        ),
        in_specs=[
            scalars,
            scalars,
            whole,
            whole,
            pl.BlockSpec((k // NX, n), lambda i: (i, 0)),
        ],
        out_specs=(
            pl.BlockSpec((NR, 1, rows, k // NX), lambda i: (0, i, 0, 0)),
            pl.BlockSpec((k // NX, n), lambda i: (i, 0)),
            pl.BlockSpec((NR, rows, n), lambda i: (0, 0, 0)),
        ),
        compiler_params=pltpu.CompilerParams(vmem_limit_bytes=VMEM),
        cost_estimate=pl.CostEstimate(
            flops=4 * half * rows * n * k,
            bytes_accessed=4 * half * rows * k,
            transcendentals=0,
        ),
    )(place, scales, near, far, values)


def sum_kernel(z, parts, ahead, behind, across, kept):
    def of(s):
        at = lax.rem(z[0] + s, NZ)
        total = parts[at, 0].astype(F32)
        for i in range(1, NX):
            total = total + parts[at, i].astype(F32)
        return total

    for i, (near, far) in enumerate(((1, 7), (3, 5))):
        ahead[i] = of(near).astype(BF)
        behind[i] = of(far).astype(BF)
    across[...] = of(4).astype(BF)
    for i, s in enumerate((0, 2, 6)):
        kept[i] = of(s)


def sum_over_x(z, parts):
    _, _, rows, k = parts.shape
    vmem = pl.BlockSpec(memory_space=pltpu.VMEM)
    return pl.pallas_call(
        sum_kernel,
        out_shape=(
            jax.ShapeDtypeStruct((2, rows, k), BF),
            jax.ShapeDtypeStruct((2, rows, k), BF),
            jax.ShapeDtypeStruct((rows, k), BF),
            jax.ShapeDtypeStruct((3, rows, k), F32),
        ),
        in_specs=[pl.BlockSpec(memory_space=pltpu.SMEM), vmem],
        out_specs=(vmem,) * 4,
        compiler_params=pltpu.CompilerParams(vmem_limit_bytes=VMEM),
        cost_estimate=pl.CostEstimate(
            flops=NZ * NX * rows * k, bytes_accessed=12 * NZ * rows * k, transcendentals=0
        ),
    )(z.reshape(1), parts)


def assemble_kernel(x, *refs):
    parts, out = refs[:NX], refs[NX]
    n = parts[0].shape[1]
    for off in range(NX):
        at = pl.multiple_of(lax.rem(x[0] + off, NX) * n, 128)
        out[:, pl.ds(at, n)] = parts[off][...]


def assemble(x, parts):
    t, n = parts[0].shape
    return pl.pallas_call(
        assemble_kernel,
        out_shape=jax.ShapeDtypeStruct((t, NX * n), BF),
        in_specs=[pl.BlockSpec(memory_space=pltpu.SMEM)]
        + [pl.BlockSpec(memory_space=pltpu.VMEM)] * NX,
        out_specs=pl.BlockSpec(memory_space=pltpu.VMEM),
        cost_estimate=pl.CostEstimate(
            flops=0, bytes_accessed=4 * t * NX * n, transcendentals=0
        ),
    )(x.reshape(1), *parts)


def together(*values):
    return lax.optimization_barrier(values)


def per_device(act_values, act_scales, weight_values, weight_scales, cotangent):
    r, z, x = (lax.axis_index(a) for a in ("r", "z", "x"))
    t, n = cotangent.shape

    act = dequantize_rows(act_values, act_scales)
    act, cotangent = together(act, cotangent)
    here = move(act, lambda r, z, x: (z, z + skew(r), x))

    turns = (0, 1, -1, 2)
    near = jnp.stack([along_y(cotangent, -k) if k else cotangent for k in turns])
    near, here = together(near, here)
    far = move(near, lambda r, z, x: (r ^ 1, z, x))
    far = pltpu.with_memory_space_constraint(far, pltpu.HBM)
    rows = [(r + NC * k) % NR ^ other for other in (0, 1) for k in turns]
    place = jnp.stack(rows + [(r + skew(row) - z) % NZ for row in rows])

    sides = [along_x(here, -1), along_x(here, 2), along_x(here, 1)]
    parts, weight, cot = grad_parts(place, near, far, weight_values, weight_scales)
    parts, *sides = together(parts, *sides)
    parts = lax.all_to_all(
        parts.reshape(NR * NX, t, n), ("r", "x"), split_axis=0, concat_axis=0, tiled=True
    )

    blocks = {0: assemble(x, [here, *sides])}
    for s in range(1, NZ // 2):
        blocks[s] = along_z(blocks[s - 1], -1)
        blocks[NZ - s] = along_z(blocks[(NZ - s + 1) % NZ], 1)
    half = t // 2
    blocks[4] = jnp.concatenate(
        [along_z(blocks[3][:half], -1), along_z(blocks[5][half:], 1)]
    )
    shares = jnp.zeros((NR, t, n), BF)
    for s in (0, 1, 7, 2, 6, 3, 5, 4):
        part = mm(blocks[s], weight).astype(BF)
        row = unskew(z + s - r)
        at = (row // NC - r // NC) % NY + (row % NC ^ r % NC) * NY
        shares = lax.dynamic_update_slice(shares, part[None], (at, 0, 0))
    both = move(shares[NY:], lambda r, z, x: (r ^ 1, z, x)).astype(F32)
    both = shares[:NY].astype(F32) + both

    ahead, behind, across, kept = sum_over_x(z, parts.reshape(NZ, NX, t, n))
    up, down, across = along_z(ahead, 1), along_z(behind, -1), along_z(across, 4)
    up2 = along_z((kept[1] + up[1].astype(F32)).astype(BF), 2)
    down2 = along_z((kept[2] + down[1].astype(F32)).astype(BF), -2)
    total = kept[0] + up[0].astype(F32) + down[0].astype(F32) + across.astype(F32)
    activation_grad = (total + up2.astype(F32) + down2.astype(F32)).astype(BF)

    parts = [along_y(both[k].astype(BF), k) for k in range(1, NY)]
    output = (both[0] + sum(part.astype(F32) for part in parts)).astype(BF)

    cot = cot.reshape(NZ, t, n)

    def grad_of(some):
        return lax.dot_general(
            jnp.concatenate([blocks[s] for s in some]),
            jnp.concatenate([cot[s] for s in some]),
            (((0,), (0,)), ((), ())),
            preferred_element_type=F32,
        )

    first = (0, 1, 7, 2, 6, 3, 5)
    for s, block in zip(first, together(*(blocks[s] for s in first))):
        blocks[s] = block
    weight_grad = grad_of(first)
    weight_grad, blocks[4] = together(weight_grad, blocks[4])
    weight_grad = (weight_grad + grad_of((4,))) * float(NR * t) ** (-0.5)
    return output, activation_grad, weight_grad


def solution(mesh):
    grid = Mesh(mesh.devices.reshape(NR, NZ, NX), ("r", "z", "x"))
    spec = P("r", ("z", "x"))
    return jax.shard_map(
        per_device,
        mesh=grid,
        in_specs=(spec,) * 5,
        out_specs=(spec,) * 3,
        check_vma=False,
    )
```

```python
import jax
import jax.numpy as jnp
from jax import lax
from jax.experimental import pallas as pl
from jax.experimental.pallas import tpu as pltpu
from jax.sharding import Mesh
from jax.sharding import PartitionSpec as P

NR, NC, NY, NZ, NX = 8, 2, 4, 8, 4
BF, F32 = jnp.bfloat16, jnp.float32
BLOCK = 128
VMEM = 16 * 1024 * 1024


def dequantize_rows(values, scales):
    blocks = (
        values.astype(F32).reshape(values.shape[0], scales.shape[1], -1)
        * scales[:, :, None]
    )
    return blocks.reshape(values.shape).astype(BF)


def skew(r):
    return r // NC + r % NC * (NR // NC)


def unskew(d):
    d = d % NZ
    return d % (NR // NC) * NC + d // (NR // NC)


def move(value, where):
    pairs = []
    for r in range(NR):
        for z in range(NZ):
            for x in range(NX):
                r2, z2, x2 = where(r, z, x)
                to = ((r2 % NR) * NZ + z2 % NZ) * NX + x2 % NX
                pairs.append(((r * NZ + z) * NX + x, to))
    return lax.ppermute(value, ("r", "z", "x"), pairs)


def along_x(value, k):
    return move(value, lambda r, z, x: (r, z, x + k))


def along_y(value, k):
    return move(value, lambda r, z, x: (r + NC * k, z, x))


def along_z(value, k):
    return move(value, lambda r, z, x: (r, z + k, x))


def mm(a, b):
    return jnp.dot(a, b, preferred_element_type=F32)


def grad_kernel(place, scales, near, far, values, parts, weight, cot):
    at = pl.program_id(0)
    for i in range(values.shape[0] // BLOCK):
        for j in range(values.shape[1] // BLOCK):
            rows, cols = pl.ds(i * BLOCK, BLOCK), pl.ds(j * BLOCK, BLOCK)
            scale = scales[at * (values.shape[0] // BLOCK) + i, j]
            weight[rows, cols] = (values[rows, cols].astype(F32) * scale).astype(BF)
    half, rows, n = near.shape
    for h, some in enumerate((near, far)):
        part = lax.dot_general(
            some[...].reshape(half * rows, n),
            weight[...],
            (((1,), (1,)), ((), ())),
            preferred_element_type=F32,
        ).astype(BF)
        for i in range(half):
            parts[place[h * half + i], 0] = part[i * rows : (i + 1) * rows]

    @pl.when(at == 0)
    def _():
        for h, some in enumerate((near, far)):
            for i in range(half):
                cot[place[NR + h * half + i]] = some[i]


def grad_parts(place, near, far, values, scales):
    half, rows, n = near.shape
    k = values.shape[0]
    whole = pl.BlockSpec((half, rows, n), lambda i: (0, 0, 0))
    scalars = pl.BlockSpec(memory_space=pltpu.SMEM)
    return pl.pallas_call(
        grad_kernel,
        grid=(NX,),
        out_shape=(
            pltpu.HBM((NR, NX, rows, k // NX), BF),
            jax.ShapeDtypeStruct((k, n), BF),
            jax.ShapeDtypeStruct((NR, rows, n), BF),
        ),
        in_specs=[
            scalars,
            scalars,
            whole,
            whole,
            pl.BlockSpec((k // NX, n), lambda i: (i, 0)),
        ],
        out_specs=(
            pl.BlockSpec((NR, 1, rows, k // NX), lambda i: (0, i, 0, 0)),
            pl.BlockSpec((k // NX, n), lambda i: (i, 0)),
            pl.BlockSpec((NR, rows, n), lambda i: (0, 0, 0)),
        ),
        compiler_params=pltpu.CompilerParams(vmem_limit_bytes=VMEM),
        cost_estimate=pl.CostEstimate(
            flops=4 * half * rows * n * k,
            bytes_accessed=4 * half * rows * k,
            transcendentals=0,
        ),
    )(place, scales, near, far, values)


def sum_kernel(z, parts, ahead, behind, across, kept):
    def of(s):
        at = lax.rem(z[0] + s, NZ)
        total = parts[at, 0].astype(F32)
        for i in range(1, NX):
            total = total + parts[at, i].astype(F32)
        return total

    for i, (near, far) in enumerate(((1, 7), (3, 5))):
        ahead[i] = of(near).astype(BF)
        behind[i] = of(far).astype(BF)
    across[...] = of(4).astype(BF)
    for i, s in enumerate((0, 2, 6)):
        kept[i] = of(s)


def sum_over_x(z, parts):
    _, _, rows, k = parts.shape
    vmem = pl.BlockSpec(memory_space=pltpu.VMEM)
    return pl.pallas_call(
        sum_kernel,
        out_shape=(
            jax.ShapeDtypeStruct((2, rows, k), BF),
            jax.ShapeDtypeStruct((2, rows, k), BF),
            jax.ShapeDtypeStruct((rows, k), BF),
            jax.ShapeDtypeStruct((3, rows, k), F32),
        ),
        in_specs=[pl.BlockSpec(memory_space=pltpu.SMEM), vmem],
        out_specs=(vmem,) * 4,
        compiler_params=pltpu.CompilerParams(vmem_limit_bytes=VMEM),
        cost_estimate=pl.CostEstimate(
            flops=NZ * NX * rows * k, bytes_accessed=12 * NZ * rows * k, transcendentals=0
        ),
    )(z.reshape(1), parts)


def assemble_kernel(x, *refs):
    parts, out, sems = refs[:NX], refs[NX], refs[NX + 1]
    n = parts[0].shape[1]
    copies = []
    for off in range(NX):
        at = pl.multiple_of(lax.rem(x[0] + off, NX) * n, 128)
        copies.append(
            pltpu.make_async_copy(parts[off], out.at[:, pl.ds(at, n)], sems.at[off])
        )
        copies[-1].start()
    for copy in copies:
        copy.wait()


def assemble(x, parts):
    t, n = parts[0].shape
    return pl.pallas_call(
        assemble_kernel,
        out_shape=jax.ShapeDtypeStruct((t, NX * n), BF),
        in_specs=[pl.BlockSpec(memory_space=pltpu.SMEM)]
        + [pl.BlockSpec(memory_space=pl.ANY)] * NX,
        out_specs=pl.BlockSpec(memory_space=pl.ANY),
        scratch_shapes=[pltpu.SemaphoreType.DMA((NX,))],
        cost_estimate=pl.CostEstimate(
            flops=0, bytes_accessed=4 * t * NX * n, transcendentals=0
        ),
    )(x.reshape(1), *parts)


def together(*values):
    return lax.optimization_barrier(values)


def per_device(act_values, act_scales, weight_values, weight_scales, cotangent):
    r, z, x = (lax.axis_index(a) for a in ("r", "z", "x"))
    t, n = cotangent.shape

    act = dequantize_rows(act_values, act_scales)
    act, cotangent = together(act, cotangent)
    here = move(act, lambda r, z, x: (z, z + skew(r), x))

    turns = (0, 1, -1, 2)
    near = jnp.stack([along_y(cotangent, -k) if k else cotangent for k in turns])
    near, here = together(near, here)
    far = move(near, lambda r, z, x: (r ^ 1, z, x))
    far = pltpu.with_memory_space_constraint(far, pltpu.HBM)
    rows = [(r + NC * k) % NR ^ other for other in (0, 1) for k in turns]
    place = jnp.stack(rows + [(r + skew(row) - z) % NZ for row in rows])

    sides = [along_x(here, -1), along_x(here, 2), along_x(here, 1)]
    parts, weight, cot = grad_parts(place, near, far, weight_values, weight_scales)
    parts, *sides = together(parts, *sides)
    parts = lax.all_to_all(
        parts.reshape(NR * NX, t, n), ("r", "x"), split_axis=0, concat_axis=0, tiled=True
    )

    blocks = {0: assemble(x, [here, *sides])}
    for s in range(1, NZ // 2):
        blocks[s] = along_z(blocks[s - 1], -1)
        blocks[NZ - s] = along_z(blocks[(NZ - s + 1) % NZ], 1)
    half = t // 2
    blocks[4] = jnp.concatenate(
        [along_z(blocks[3][:half], -1), along_z(blocks[5][half:], 1)]
    )
    shares = jnp.zeros((NR, t, n), BF)
    for s in (0, 1, 7, 2, 6, 3, 5, 4):
        part = mm(blocks[s], weight).astype(BF)
        row = unskew(z + s - r)
        at = (row // NC - r // NC) % NY + (row % NC ^ r % NC) * NY
        shares = lax.dynamic_update_slice(shares, part[None], (at, 0, 0))
    both = move(shares[NY:], lambda r, z, x: (r ^ 1, z, x)).astype(F32)
    both = shares[:NY].astype(F32) + both

    ahead, behind, across, kept = sum_over_x(z, parts.reshape(NZ, NX, t, n))
    up, down, across = along_z(ahead, 1), along_z(behind, -1), along_z(across, 4)
    up2 = along_z((kept[1] + up[1].astype(F32)).astype(BF), 2)
    down2 = along_z((kept[2] + down[1].astype(F32)).astype(BF), -2)
    total = kept[0] + up[0].astype(F32) + down[0].astype(F32) + across.astype(F32)
    activation_grad = (total + up2.astype(F32) + down2.astype(F32)).astype(BF)

    parts = [along_y(both[k].astype(BF), k) for k in range(1, NY)]
    output = (both[0] + sum(part.astype(F32) for part in parts)).astype(BF)

    cot = cot.reshape(NZ, t, n)

    def grad_of(some):
        return lax.dot_general(
            jnp.concatenate([blocks[s] for s in some]),
            jnp.concatenate([cot[s] for s in some]),
            (((0,), (0,)), ((), ())),
            preferred_element_type=F32,
        )

    first = (0, 1, 7, 2, 6, 3, 5)
    for s, block in zip(first, together(*(blocks[s] for s in first))):
        blocks[s] = block
    weight_grad = grad_of(first)
    weight_grad, blocks[4] = together(weight_grad, blocks[4])
    weight_grad = (weight_grad + grad_of((4,))) * float(NR * t) ** (-0.5)
    return output, activation_grad, weight_grad


def solution(mesh):
    grid = Mesh(mesh.devices.reshape(NR, NZ, NX), ("r", "z", "x"))
    spec = P("r", ("z", "x"))
    return jax.shard_map(
        per_device,
        mesh=grid,
        in_specs=(spec,) * 5,
        out_specs=(spec,) * 3,
        check_vma=False,
    )
```
